32 devices in a mesh: role: 2 (over x), dp: 2 (over core), hidden: 8 (over z, y).
Axes of the slice: x: 2, y: 2, z: 4, core: 2. Of those that a mesh axis runs over, the one named last changes fastest.
Arguments:
- token_rows: bfloat16 [2, 256, 5120], P('role', 'dp'), may hold values from -6 to 6
- cotangent: bfloat16 [256, 5120], P('dp'), may hold values from -6 to 6
- staleness: int32 [256], P('dp'), may hold values from 0 to 7
- prefill_rows: int32 [2], P('dp'), may hold values from 1 to 128, as said below
- frozen_gate_up_weight: bfloat16 [2, 5120, 13824], P(None, ('role', 'dp'), 'hidden'), may hold values from -0.078125 to 0.078125
- down_weight: bfloat16 [13824, 5120], P('hidden', ('role', 'dp')), may hold values from -0.0546875 to 0.0546875
- adapter_in: float32 [2, 5120, 32], P(None, 'hidden'), may hold values from -0.078125 to 0.078125
- adapter_out: float32 [2, 32, 13824], P(None, None, 'hidden'), may hold values from -0.6 to 0.6
- moment_in: float32 [2, 5120, 32], P(None, 'hidden'), may hold values from -274.76804 to 274.76804
- square_in: float32 [2, 5120, 32], P(None, 'hidden'), may hold values from 5.24288 to 524.288
- moment_out: float32 [2, 32, 13824], P(None, None, 'hidden'), may hold values from -1.2 to 1.2
- square_out: float32 [2, 32, 13824], P(None, None, 'hidden'), may hold values from 0.01 to 1
Outputs:
- layer_old: bfloat16 [2, 256, 5120], P('role', 'dp', 'hidden')
- layer_new: bfloat16 [2, 256, 5120], P('role', 'dp', 'hidden')
- new_adapter_in: float32 [2, 2, 5120, 32], P('role', None, 'hidden')
- new_adapter_out: float32 [2, 2, 32, 13824], P('role', None, None, 'hidden')
- new_moment_in: float32 [2, 2, 5120, 32], P('role', None, 'hidden')
- new_square_in: float32 [2, 2, 5120, 32], P('role', None, 'hidden')
- new_moment_out: float32 [2, 2, 32, 13824], P('role', None, None, 'hidden')
- new_square_out: float32 [2, 2, 32, 13824], P('role', None, None, 'hidden')
The draws below stay inside these ranges and needn't reach their ends.
Inputs may be any that keep to these rules, and one draw needn't show every extreme that they name: The first prefill_rows[g] rows of rollout group g are live, the rest are padding; some group is full in every draw.
All inputs are finite; a program needn't handle non-finite values.
Results may differ from the reference program's by a relative error of at most 0.025.
Values may be sent and summed in bfloat16 or wider, within the bound.
A program may use at most 128 MiB of HBM per device.

```python
import math
import jax
import jax.numpy as jnp
from jax import lax

D = 5120
FF = 13824
R = 32
GROUP_ROWS = 128
OPT_STEP = 10
ROWS = 256
N_DP = 2
N_HIDDEN = 8


def draw_prefill_rows(key, part):
    base = jax.random.fold_in(key, 11)
    first_key, second_key = jax.random.split(base)
    counts = jax.random.randint(first_key, (N_DP,), 1, GROUP_ROWS + 1)
    full_group = jax.random.randint(second_key, (), 0, N_DP)
    return jnp.where(jnp.arange(N_DP) == full_group, GROUP_ROWS, counts).astype(jnp.int32)


def plant(array, own_key, least, high):
    longest = array.shape.index(max(array.shape))
    spots = []
    for shift in (0, 1):
        where = [jax.random.randint(jax.random.fold_in(own_key, axis), (), 0, length) for axis, length in enumerate(array.shape)]
        where[longest] = (where[longest] + shift) % array.shape[longest]
        spots.append(tuple(where))
    return array.at[spots[0]].set(least).at[spots[1]].set(high)


def shard_levels(own_key, extent, cuts, smallest, top_value):
    level = 1.0
    for axis_at, shards_of in cuts:
        draws = jax.random.uniform(jax.random.fold_in(jax.random.fold_in(own_key, 6), axis_at), (shards_of,), jnp.float32, smallest / len(cuts), top_value / len(cuts))
        level = level * jnp.repeat(jnp.exp(draws), extent[axis_at] // shards_of).reshape((-1,) + (1,) * (len(extent) - 1 - axis_at))
    return level


def centred(rng, shape, deviation, most, cuts=(), kind=jnp.bfloat16):
    values = deviation * jax.random.normal(rng, shape, jnp.float32)
    if cuts:
        values = values * shard_levels(rng, shape, cuts, -0.22, 0.18)
    return jnp.clip(values, -most, most).astype(kind)


def setup_inputs(seed: int = 0) -> dict:
    key_of = jax.random.split(jax.random.key(seed), 13)
    token_rows = centred(key_of[0], (2, ROWS, D), 1.0, 6.0, ((0, 2), (1, 2)))
    cotangent = centred(key_of[1], (ROWS, D), 1.0, 6.0, ((0, 2),))
    staleness = plant(jax.random.randint(key_of[2], (ROWS,), 0, 8), jax.random.fold_in(key_of[2], 1), 0, 7).astype(jnp.int32)
    prefill_rows = draw_prefill_rows(jax.random.fold_in(key_of[12], 71), 0)
    frozen_gate_up_weight = centred(key_of[4], (2, D, FF), D ** -0.5, 0.078125, ((1, 4), (2, 8)))
    down_weight = centred(key_of[5], (FF, D), FF ** -0.5, 0.0546875, ((0, 8), (1, 4)))
    adapter_in = centred(key_of[6], (2, D, R), D ** -0.5, 0.078125, ((1, 8),), jnp.float32)
    adapter_out = centred(key_of[7], (2, R, FF), 0.1, 0.6, ((2, 8),), jnp.float32)
    moment_in = centred(key_of[8], (2, D, R), (0.04 * (ROWS * D) ** 0.5), 274.76804, ((1, 8),), jnp.float32)
    square_in = jnp.clip(jnp.exp(math.log(524.288) - 4.6051703 * jax.random.uniform(key_of[9], (2, D, R), jnp.float32) ** shard_levels(key_of[9], (2, D, R), ((1, 8),), -0.2, 0.2)), 5.24288, 524.288)
    moment_out = centred(key_of[10], (2, R, FF), 0.2, 1.2, ((2, 8),), jnp.float32)
    square_out = jnp.clip(jnp.exp(math.log(1.0) - 4.6051702 * jax.random.uniform(key_of[11], (2, R, FF), jnp.float32) ** shard_levels(key_of[11], (2, R, FF), ((2, 8),), -0.2, 0.2)), 0.01, 1.0)
    return dict(token_rows=token_rows, cotangent=cotangent, staleness=staleness, prefill_rows=prefill_rows, frozen_gate_up_weight=frozen_gate_up_weight, down_weight=down_weight, adapter_in=adapter_in, adapter_out=adapter_out, moment_in=moment_in, square_in=square_in, moment_out=moment_out, square_out=square_out)


ADAPTER_SCALE = 2.0
BETA_ONE = 0.9
BETA_TWO = 0.999
RATE_FACTOR = 0.34
ADAM_EPS = 1e-08
KEEP_RATE = 0.75

def adam_update(param, grad, first, second):
    learn_rate = RATE_FACTOR / D ** 0.5
    first_new = BETA_ONE * first + (1.0 - BETA_ONE) * grad
    second_new = BETA_TWO * second + (1.0 - BETA_TWO) * grad * grad
    first_fix = first_new / (1.0 - BETA_ONE ** OPT_STEP)
    second_fix = second_new / (1.0 - BETA_TWO ** OPT_STEP)
    return (param - learn_rate * first_fix / (jnp.sqrt(second_fix) + ADAM_EPS), first_new, second_new)

def down_sum(hidden_act, down_weight):
    width = FF // N_HIDDEN
    total = jnp.zeros((hidden_act.shape[0], D), jnp.float32)
    for segment in range(N_HIDDEN):
        partial_value = jnp.dot(hidden_act[:, segment * width:(segment + 1) * width], down_weight[segment * width:(segment + 1) * width], preferred_element_type=jnp.float32)
        rounded = lax.optimization_barrier(partial_value.astype(jnp.bfloat16))
        total = total + rounded.astype(jnp.float32)
    return total.astype(jnp.bfloat16)

def twice(value):
    return jnp.stack([value, value])

def reference(token_rows, cotangent, staleness, prefill_rows, frozen_gate_up_weight, down_weight, adapter_in, adapter_out, moment_in, square_in, moment_out, square_out):
    in_bf = adapter_in.astype(jnp.bfloat16)
    out_bf = adapter_out.astype(jnp.bfloat16)
    positions = jnp.arange(ROWS)
    limit = jnp.take(prefill_rows, positions // GROUP_ROWS)
    live = positions % GROUP_ROWS < limit
    old_list = []
    for half in range(2):
        token_batch = token_rows[half]
        reduced_gradient = jnp.einsum('rd,kdq->krq', token_batch.astype(jnp.float32), in_bf.astype(jnp.float32)).astype(jnp.bfloat16)
        lifted_rows = jnp.einsum('krq,kqf->krf', reduced_gradient.astype(jnp.float32), out_bf.astype(jnp.float32))
        gate_preactivation = jnp.dot(token_batch, frozen_gate_up_weight[0], preferred_element_type=jnp.float32) + ADAPTER_SCALE * lifted_rows[0]
        up_preactivation = jnp.dot(token_batch, frozen_gate_up_weight[1], preferred_element_type=jnp.float32) + ADAPTER_SCALE * lifted_rows[1]
        hidden_act = (jax.nn.silu(gate_preactivation) * up_preactivation).astype(jnp.bfloat16)
        result = down_sum(hidden_act, down_weight)
        if half == 1:
            result = jnp.where(live[:, None], result, jnp.zeros_like(result))
        else:
            saved = (token_batch, reduced_gradient, gate_preactivation, up_preactivation)
        old_list.append(result)
    token_batch, reduced_gradient, gate_preactivation, up_preactivation = saved
    row_weight = KEEP_RATE ** staleness.astype(jnp.float32)
    upstream = (row_weight[:, None] * cotangent.astype(jnp.float32)).astype(jnp.bfloat16)
    grad_hidden = lax.dot_general(upstream, down_weight, (((1,), (1,)), ((), ())), preferred_element_type=jnp.float32)
    sigma = jax.nn.sigmoid(gate_preactivation)
    grad_gate = (grad_hidden * up_preactivation * sigma * (1.0 + gate_preactivation * (1.0 - sigma))).astype(jnp.bfloat16)
    grad_up = (grad_hidden * gate_preactivation * sigma).astype(jnp.bfloat16)
    gradient_tree = jnp.stack([grad_gate, grad_up]).astype(jnp.float32)
    adapter_out_gradient = ADAPTER_SCALE * jnp.einsum('aod,aot->adt', reduced_gradient.astype(jnp.float32), gradient_tree)
    passed_through = jnp.einsum('krf,kqf->krq', gradient_tree, out_bf.astype(jnp.float32)).astype(jnp.bfloat16)
    adapter_in_gradient = ADAPTER_SCALE * jnp.einsum('un,huj->hnj', token_batch.astype(jnp.float32), passed_through.astype(jnp.float32))
    new_in, new_m_in, new_s_in = adam_update(adapter_in, adapter_in_gradient, moment_in, square_in)
    new_out, new_m_out, new_s_out = adam_update(adapter_out, adapter_out_gradient, moment_out, square_out)
    updated_in_brainfloat = new_in.astype(jnp.bfloat16)
    updated_out_brainfloat = new_out.astype(jnp.bfloat16)
    merged_weight = []
    for group_member in range(2):
        merged_weight.append((frozen_gate_up_weight[group_member].astype(jnp.float32) + ADAPTER_SCALE * jnp.dot(updated_in_brainfloat[group_member], updated_out_brainfloat[group_member], preferred_element_type=jnp.float32)).astype(jnp.bfloat16))
    new_list = []
    for half in range(2):
        token_batch = token_rows[half]
        gate_post = jnp.dot(token_batch, merged_weight[0], preferred_element_type=jnp.float32)
        up_post = jnp.dot(token_batch, merged_weight[1], preferred_element_type=jnp.float32)
        hidden_act = (jax.nn.silu(gate_post) * up_post).astype(jnp.bfloat16)
        result = down_sum(hidden_act, down_weight)
        if half == 1:
            result = jnp.where(live[:, None], result, jnp.zeros_like(result))
        new_list.append(result)
    return (jnp.stack(old_list), jnp.stack(new_list), twice(new_in), twice(new_out), twice(new_m_in), twice(new_s_in), twice(new_m_out), twice(new_s_out))
```

```python
import functools

import jax
import jax.numpy as jnp
from jax import lax
from jax.experimental import pallas as pl
from jax.experimental.pallas import tpu as pltpu
from jax.sharding import PartitionSpec as P

OPT_STEP = 10
ADAPTER_SCALE = 2.0
BETA_ONE = 0.9
BETA_TWO = 0.999
RATE_FACTOR = 0.34
ADAM_EPS = 1e-08
KEEP_RATE = 0.75

MESH = pl.DeviceIdType.MESH
VMEM_LIMIT = 48 * 1024 * 1024
F32 = jnp.float32
BF16 = jnp.bfloat16


def adam_update(param, grad, first, second, width):
    learn_rate = RATE_FACTOR / width**0.5
    first_new = BETA_ONE * first + (1.0 - BETA_ONE) * grad
    second_new = BETA_TWO * second + (1.0 - BETA_TWO) * grad * grad
    first_fix = first_new / (1.0 - BETA_ONE**OPT_STEP)
    second_fix = second_new / (1.0 - BETA_TWO**OPT_STEP)
    return (
        param - learn_rate * first_fix / (jnp.sqrt(second_fix) + ADAM_EPS),
        first_new,
        second_new,
    )


def shape_of(shape, dtype):
    return jax.ShapeDtypeStruct(shape, dtype)


def ring(index, step, size):
    return lax.rem(index + step, size)


def remote(src, dst, sems, slot, device):
    send, recv = sems
    return pltpu.make_async_remote_copy(
        src_ref=src,
        dst_ref=dst,
        send_sem=send.at[slot],
        recv_sem=recv.at[slot],
        device_id=device,
        device_id_type=MESH,
    )


def greet(peers):
    barrier = pltpu.get_barrier_semaphore()
    for peer in peers:
        pl.semaphore_signal(barrier, inc=1, device_id=peer, device_id_type=MESH)
    pl.semaphore_wait(barrier, len(peers))


def hidden_peers(hidden):
    me = lax.axis_index("hidden")
    return [{"hidden": ring(me, step, hidden)} for step in range(1, hidden)]


def dp_peers(n_dp):
    me = lax.axis_index("dp")
    return [{"dp": ring(me, step, n_dp)} for step in range(1, n_dp)]


def other_role():
    return {"role": 1 - lax.axis_index("role")}


def call(body, outs, scratch, cid, *operands):
    spec = pl.BlockSpec(memory_space=pltpu.VMEM)
    return pl.pallas_call(
        body,
        out_shape=outs,
        in_specs=[spec] * len(operands),
        out_specs=[spec] * len(outs),
        scratch_shapes=scratch,
        compiler_params=pltpu.CompilerParams(
            collective_id=cid, has_side_effects=True, vmem_limit_bytes=VMEM_LIMIT
        ),
    )(*operands)


def dma_pair(count):
    return [pltpu.SemaphoreType.DMA((count,)), pltpu.SemaphoreType.DMA((count,))]


def spread_kernel(sizes, tok, up, red, tok_all, up_all, red_all, s0, r0, s1, r1, s2, r2):
    n_role, n_dp, hidden = sizes
    role, dp, me = (lax.axis_index(a) for a in ("role", "dp", "hidden"))
    group = [
        (ring(role, a, n_role), ring(dp, b, n_dp))
        for a in range(n_role)
        for b in range(n_dp)
        if a or b
    ]
    greet([{"role": a, "dp": b} for a, b in group] + hidden_peers(hidden))
    copies = []
    own = dp * n_role + role
    for slot, (a, b) in enumerate(group):
        copies.append(
            remote(tok.at[a * n_dp + b], tok_all.at[own], (s0, r0), slot, {"role": a, "dp": b})
        )
    for slot, peer in enumerate(dp_peers(n_dp)):
        copies.append(remote(up.at[role * n_dp + peer["dp"]], up_all.at[dp], (s1, r1), slot, peer))
    for slot, peer in enumerate(hidden_peers(hidden)):
        copies.append(remote(red, red_all.at[me], (s2, r2), slot, peer))
    for copy in copies:
        copy.start()
    tok_all[own] = tok[role * n_dp + dp]
    up_all[dp] = up[role * n_dp + dp]
    red_all[me] = red[...]
    for copy in copies:
        copy.wait()


def reduce_kernel(sizes, part, grad, base, grad_sum, got, got_grad, out_part, out_grad, far, far_grad,
                  s0, r0, s1, r1, s2, r2, s3, r3):
    n_role, n_dp, _ = sizes
    role, dp = lax.axis_index("role"), lax.axis_index("dp")
    greet(dp_peers(n_dp) + [other_role()])
    copies = []
    for slot, peer in enumerate(dp_peers(n_dp)):
        copies.append(remote(part.at[:, peer["dp"]], got.at[slot], (s0, r0), slot, peer))
        copies.append(remote(grad.at[peer["dp"]], got_grad.at[slot], (s1, r1), slot, peer))
    for copy in copies:
        copy.start()
    for copy in copies:
        copy.wait()
    rows = base.shape[1]
    step = 16

    @pl.loop(0, rows // step)
    def _(i):
        at = pl.ds(pl.multiple_of(i * step, step), step)
        for k in range(2):
            total = part[k, dp, 1 - role, at].astype(F32)
            for slot in range(n_dp - 1):
                total = total + got[slot, k, 1 - role, at].astype(F32)
            out_part[k, at] = total.astype(BF16)
        total = grad[dp, at].astype(F32)
        for slot in range(n_dp - 1):
            total = total + got_grad[slot, at].astype(F32)
        out_grad[at] = total.astype(BF16)

    across = remote(out_part, far, (s2, r2), 0, other_role())
    across_grad = remote(out_grad, far_grad, (s3, r3), 0, other_role())
    across.start()

    @pl.when(role == 1)
    def _():
        across_grad.start()
        across_grad.wait_send()

    @pl.when(role == 0)
    def _():
        across_grad.wait_recv()

    across.wait()
    keep = jnp.where(role == 0, 1.0, 0.0).astype(F32)

    @pl.loop(0, rows // step)
    def _(i):
        at = pl.ds(pl.multiple_of(i * step, step), step)
        for k in range(2):
            total = part[k, dp, role, at].astype(F32)
            for slot in range(n_dp - 1):
                total = total + got[slot, k, role, at].astype(F32)
            base[k, at] = total + far[k, at].astype(F32)

        @pl.when(role == 0)
        def _():
            grad_sum[at] = out_grad[at].astype(F32) + far_grad[at].astype(F32)

        @pl.when(role == 1)
        def _():
            grad_sum[at] = jnp.zeros_like(grad_sum[at])


def share_kernel(sizes, with_hidden, with_gather, with_grad, *refs):
    n_role, n_dp, hidden = sizes
    role, dp, me = (lax.axis_index(a) for a in ("role", "dp", "hidden"))
    refs = list(refs)
    n_jobs = with_hidden + with_gather + with_grad
    ins, outs, sems = refs[:n_jobs], refs[n_jobs : 2 * n_jobs], refs[2 * n_jobs :]
    peers = []
    if with_hidden:
        peers += hidden_peers(hidden)
    if with_gather or with_grad:
        peers += dp_peers(n_dp) + [other_role()]
    greet(peers)
    waits = []
    if with_hidden:
        src, dst, pair = ins.pop(0), outs.pop(0), (sems.pop(0), sems.pop(0))
        for slot, peer in enumerate(hidden_peers(hidden)):
            copy = remote(src, dst.at[me], pair, slot, peer)
            copy.start()
            waits.append(copy)
        dst[me] = src[...]
    if with_grad:
        grad_src, grad_dst = ins.pop(), outs.pop()
        g_near, g_far = (sems.pop(-2), sems.pop()), (sems.pop(-2), sems.pop())
        grad_over = remote(grad_src, grad_dst.at[dp], g_far, 0, other_role())

        @pl.when(role == 0)
        def _():
            grad_over.start()
            grad_dst[dp] = grad_src[...]

    if with_gather:
        src, dst = ins.pop(0), outs.pop(0)
        near, far = (sems.pop(0), sems.pop(0)), (sems.pop(0), sems.pop(0))
        over = remote(src, dst.at[dp, role], far, 0, other_role())
        over.start()
        dst[dp, role] = src[...]
    if with_grad:

        @pl.when(role == 0)
        def _():
            grad_over.wait_send()

        @pl.when(role == 1)
        def _():
            grad_over.wait_recv()

        for slot, peer in enumerate(dp_peers(n_dp)):
            copy = remote(grad_dst.at[dp], grad_dst.at[dp], g_near, slot, peer)
            copy.start()
            waits.append(copy)
    if with_gather:
        over.wait()
        for slot, peer in enumerate(dp_peers(n_dp)):
            copy = remote(dst.at[dp], dst.at[dp], near, slot, peer)
            copy.start()
            waits.append(copy)
    for copy in waits:
        copy.wait()


def share(sizes, cid, hidden_in=None, gather_in=None, grad_in=None):
    n_role, n_dp, hidden = sizes
    operands, outs, scratch = [], [], []
    if hidden_in is not None:
        operands.append(hidden_in)
        outs.append(shape_of((hidden,) + hidden_in.shape, hidden_in.dtype))
        scratch += dma_pair(hidden - 1)
    if gather_in is not None:
        operands.append(gather_in)
        outs.append(shape_of((n_dp, n_role) + gather_in.shape, gather_in.dtype))
        scratch += dma_pair(n_dp - 1) + dma_pair(1)
    if grad_in is not None:
        operands.append(grad_in)
        outs.append(shape_of((n_dp,) + grad_in.shape, grad_in.dtype))
        scratch += dma_pair(1) + dma_pair(n_dp - 1)
    body = functools.partial(
        share_kernel, sizes, hidden_in is not None, gather_in is not None, grad_in is not None
    )
    return call(body, outs, scratch, cid, *operands)


def finish_kernel(sizes, part, out, got, summed, far, result, s0, r0, s1, r1, s2, r2):
    n_role, n_dp, hidden = sizes
    role, dp, me = (lax.axis_index(a) for a in ("role", "dp", "hidden"))
    pairs = hidden // 2
    pair, odd = me // 2, lax.rem(me, 2)
    mine = role * n_dp + dp
    t_role, t_dp = pair // n_dp, lax.rem(pair, n_dp)
    owner = {"role": t_role, "dp": t_dp, "hidden": mine * 2 + odd}
    others = [{"hidden": ring(pair, step, pairs) * 2 + odd} for step in range(1, pairs)]
    mate = {"hidden": pair * 2 + 1 - odd}
    barrier = pltpu.get_barrier_semaphore()
    for peer in others + [mate]:
        pl.semaphore_signal(barrier, inc=1, device_id=peer, device_id_type=MESH)

    @pl.when(mine != pair)
    def _():
        pl.semaphore_signal(barrier, inc=1, device_id=owner, device_id_type=MESH)

    pl.semaphore_wait(barrier, jnp.where(mine != pair, pairs + 1, pairs))

    order = list(range(1, pairs)) + [0]
    firsts = []
    for step in order:
        block = ring(pair, step, pairs)
        copy = remote(part.at[block, 1 - odd], got.at[block], (s0, r0), step, mate)
        firsts.append((step, block, copy))
    for _, _, copy in firsts:
        copy.start()
    seconds = []
    for step, block, copy in firsts:
        copy.wait()
        total = part[block, odd].astype(F32) + got[block].astype(F32)
        summed[block] = total.astype(BF16)
        if step:
            copy = remote(summed.at[block], far.at[step - 1], (s1, r1), step - 1, others[step - 1])
            copy.start()
            seconds.append(copy)
    total = summed[pair].astype(F32)
    for step, copy in enumerate(seconds):
        copy.wait()
        total = total + far[step].astype(F32)
    result[...] = total.astype(BF16)
    last = remote(result, out, (s2, r2), 0, owner)

    @pl.when(mine != pair)
    def _():
        last.start()
        last.wait()

    @pl.when(mine == pair)
    def _():
        out[...] = result[...]


def finish(sizes, cid, hidden_all, down_weight, live):
    n_role, n_dp, hidden = sizes
    rows = hidden_all.shape[2]
    width = down_weight.shape[1]
    per = hidden // (n_role * n_dp)
    part = jnp.einsum("grf,fd->grd", hidden_all.reshape((-1,) + hidden_all.shape[2:]), down_weight,
                      preferred_element_type=F32).astype(BF16)
    part = part.reshape(n_dp, n_role, rows, per, width // per)
    part = part.transpose(1, 0, 3, 2, 4).reshape(n_role * n_dp, per, rows, width // per)
    pairs = hidden // 2
    block = (rows, width // per)
    (out,) = call(
        functools.partial(finish_kernel, sizes),
        [shape_of(block, BF16)],
        [
            pltpu.VMEM((pairs,) + block, BF16),
            pltpu.VMEM((pairs,) + block, BF16),
            pltpu.VMEM((pairs - 1,) + block, BF16),
            pltpu.VMEM(block, BF16),
        ]
        + dma_pair(pairs)
        + dma_pair(pairs - 1)
        + dma_pair(1),
        cid,
        part,
    )
    return jnp.where(live[:, None], out, jnp.zeros_like(out))


def local(
    sizes,
    token_rows,
    cotangent,
    staleness,
    prefill_rows,
    frozen_gate_up_weight,
    down_weight,
    adapter_in,
    adapter_out,
    moment_in,
    square_in,
    moment_out,
    square_out,
):
    n_role, n_dp, hidden = sizes
    groups = n_role * n_dp
    half_index = lax.axis_index("role")
    shard_index = lax.axis_index("hidden")
    token_batch = token_rows[0]
    rows, model = token_batch.shape
    part_width = adapter_in.shape[1]
    rank = adapter_in.shape[2]
    units = frozen_gate_up_weight.shape[2]
    width = frozen_gate_up_weight.shape[1]
    positions = jnp.arange(rows)
    live = jnp.logical_or(half_index == 0, positions < prefill_rows[0])

    token_part = lax.dynamic_slice_in_dim(token_batch, shard_index * part_width, part_width, 1)
    reduced_part = jnp.einsum(
        "rd,kdq->krq", token_part, adapter_in.astype(BF16), preferred_element_type=F32
    )
    row_weight = KEEP_RATE ** staleness.astype(F32)
    upstream = (row_weight[:, None] * cotangent.astype(F32)).astype(BF16)

    def blocked(value):
        return value.reshape(rows, groups, width).transpose(1, 0, 2)

    tokens_all, upstream_all, reduced_all = call(
        functools.partial(spread_kernel, sizes),
        [
            shape_of((groups, rows, width), BF16),
            shape_of((n_dp, rows, width), BF16),
            shape_of((hidden, 2, rows, rank), F32),
        ],
        dma_pair(groups - 1) + dma_pair(n_dp - 1) + dma_pair(hidden - 1),
        1,
        blocked(token_batch),
        blocked(upstream),
        reduced_part,
    )
    products = jnp.einsum(
        "rd,kdf->krf",
        tokens_all.reshape(groups * rows, width),
        frozen_gate_up_weight,
        preferred_element_type=F32,
    ).astype(BF16).reshape(2, n_dp, n_role, rows, units)
    grad_products = lax.dot_general(
        upstream_all.reshape(n_dp * rows, width),
        down_weight,
        (((1,), (1,)), ((), ())),
        preferred_element_type=F32,
    ).astype(BF16).reshape(n_dp, rows, units)
    base, grad_hidden = call(
        functools.partial(reduce_kernel, sizes),
        [shape_of((2, rows, units), F32), shape_of((rows, units), F32)],
        [
            pltpu.VMEM((n_dp - 1, 2, n_role, rows, units), BF16),
            pltpu.VMEM((n_dp - 1, rows, units), BF16),
            pltpu.VMEM((2, rows, units), BF16),
            pltpu.VMEM((rows, units), BF16),
            pltpu.VMEM((2, rows, units), BF16),
            pltpu.VMEM((rows, units), BF16),
        ]
        + dma_pair(n_dp - 1)
        + dma_pair(n_dp - 1)
        + dma_pair(1)
        + dma_pair(1),
        2,
        products,
        grad_products,
    )
    reduced = reduced_all.sum(axis=0).astype(BF16)
    out_bf = adapter_out.astype(BF16)
    pre = base + ADAPTER_SCALE * jnp.einsum(
        "krq,kqf->krf", reduced, out_bf, preferred_element_type=F32
    )
    sigma = jax.nn.sigmoid(pre[0])
    hidden_old = (pre[0] * sigma * pre[1]).astype(BF16)
    grad_gate = (grad_hidden * pre[1] * sigma * (1.0 + pre[0] * (1.0 - sigma))).astype(BF16)
    grad_up = (grad_hidden * pre[0] * sigma).astype(BF16)
    grads = jnp.stack([grad_gate, grad_up])
    partial_out = ADAPTER_SCALE * jnp.einsum(
        "krq,krf->kqf", reduced, grads, preferred_element_type=F32
    )
    through_part = jnp.einsum("krf,kqf->krq", grads, out_bf, preferred_element_type=F32)
    through_all, hidden_old_all, grad_out_all = share(
        sizes, 3, through_part, hidden_old, partial_out
    )
    through = through_all.sum(axis=0).astype(BF16)
    partial_in = ADAPTER_SCALE * jnp.einsum(
        "un,huj->hnj", token_part, through, preferred_element_type=F32
    )
    (grad_in_all,) = share(sizes, 4, None, None, partial_in)
    grad_in = grad_in_all.sum(axis=0)
    grad_out = grad_out_all.sum(axis=0)
    new_in, new_m_in, new_s_in = adam_update(adapter_in, grad_in, moment_in, square_in, model)
    new_out, new_m_out, new_s_out = adam_update(
        adapter_out, grad_out, moment_out, square_out, model
    )
    new_part = jnp.einsum(
        "rd,kdq->krq", token_part, new_in.astype(BF16), preferred_element_type=F32
    )
    (new_all,) = share(sizes, 5, new_part)
    new_reduced = new_all.sum(axis=0).astype(BF16)
    post = base + ADAPTER_SCALE * jnp.einsum(
        "krq,kqf->krf", new_reduced, new_out.astype(BF16), preferred_element_type=F32
    )
    hidden_new = (jax.nn.silu(post[0]) * post[1]).astype(BF16)
    (hidden_new_all,) = share(sizes, 6, None, hidden_new)
    layer_old = finish(sizes, 7, hidden_old_all, down_weight, live)
    layer_new = finish(sizes, 8, hidden_new_all, down_weight, live)
    return (
        layer_old[None],
        layer_new[None],
        new_in[None],
        new_out[None],
        new_m_in[None],
        new_s_in[None],
        new_m_out[None],
        new_s_out[None],
    )


def solution(mesh):
    in_specs = (
        P("role", "dp", None),
        P("dp", None),
        P("dp"),
        P("dp"),
        P(None, ("role", "dp"), "hidden"),
        P("hidden", ("role", "dp")),
        P(None, "hidden", None),
        P(None, None, "hidden"),
        P(None, "hidden", None),
        P(None, "hidden", None),
        P(None, None, "hidden"),
        P(None, None, "hidden"),
    )
    out_specs = (
        P("role", "dp", "hidden"),
        P("role", "dp", "hidden"),
        P("role", None, "hidden", None),
        P("role", None, None, "hidden"),
        P("role", None, "hidden", None),
        P("role", None, "hidden", None),
        P("role", None, None, "hidden"),
        P("role", None, None, "hidden"),
    )
    sizes = tuple(mesh.shape[axis] for axis in ("role", "dp", "hidden"))
    return jax.shard_map(
        functools.partial(local, sizes),
        mesh=mesh,
        in_specs=in_specs,
        out_specs=out_specs,
        check_vma=False,
    )
```

```python
import functools

import jax
import jax.numpy as jnp
from jax import lax
from jax.experimental import pallas as pl
from jax.experimental.pallas import tpu as pltpu
from jax.sharding import PartitionSpec as P

OPT_STEP = 10
ADAPTER_SCALE = 2.0
BETA_ONE = 0.9
BETA_TWO = 0.999
RATE_FACTOR = 0.34
ADAM_EPS = 1e-08
KEEP_RATE = 0.75

MESH = pl.DeviceIdType.MESH
VMEM_LIMIT = 48 * 1024 * 1024
F32 = jnp.float32
BF16 = jnp.bfloat16


def adam_update(param, grad, first, second, width):
    learn_rate = RATE_FACTOR / width**0.5
    first_new = BETA_ONE * first + (1.0 - BETA_ONE) * grad
    second_new = BETA_TWO * second + (1.0 - BETA_TWO) * grad * grad
    first_fix = first_new / (1.0 - BETA_ONE**OPT_STEP)
    second_fix = second_new / (1.0 - BETA_TWO**OPT_STEP)
    return (
        param - learn_rate * first_fix / (jnp.sqrt(second_fix) + ADAM_EPS),
        first_new,
        second_new,
    )


def shape_of(shape, dtype):
    return jax.ShapeDtypeStruct(shape, dtype)


def ring(index, step, size):
    return lax.rem(index + step, size)


def remote(src, dst, sems, slot, device):
    send, recv = sems
    return pltpu.make_async_remote_copy(
        src_ref=src,
        dst_ref=dst,
        send_sem=send.at[slot],
        recv_sem=recv.at[slot],
        device_id=device,
        device_id_type=MESH,
    )


def greet(peers):
    barrier = pltpu.get_barrier_semaphore()
    for peer in peers:
        pl.semaphore_signal(barrier, inc=1, device_id=peer, device_id_type=MESH)
    pl.semaphore_wait(barrier, len(peers))


def hidden_peers(hidden):
    me = lax.axis_index("hidden")
    return [{"hidden": ring(me, step, hidden)} for step in range(1, hidden)]


def dp_peers(n_dp):
    me = lax.axis_index("dp")
    return [{"dp": ring(me, step, n_dp)} for step in range(1, n_dp)]


def other_role():
    return {"role": 1 - lax.axis_index("role")}


def call(body, outs, scratch, cid, *operands):
    spec = pl.BlockSpec(memory_space=pltpu.VMEM)
    return pl.pallas_call(
        body,
        out_shape=outs,
        in_specs=[spec] * len(operands),
        out_specs=[spec] * len(outs),
        scratch_shapes=scratch,
        compiler_params=pltpu.CompilerParams(
            collective_id=cid, has_side_effects=True, vmem_limit_bytes=VMEM_LIMIT
        ),
    )(*operands)


def dma_pair(count):
    return [pltpu.SemaphoreType.DMA((count,)), pltpu.SemaphoreType.DMA((count,))]


def spread_kernel(sizes, tok, up, red, tok_all, up_all, red_all, s0, r0, s1, r1, s2, r2):
    n_role, n_dp, hidden = sizes
    role, dp, me = (lax.axis_index(a) for a in ("role", "dp", "hidden"))
    group = [
        (ring(role, a, n_role), ring(dp, b, n_dp))
        for a in range(n_role)
        for b in range(n_dp)
        if a or b
    ]
    greet([{"role": a, "dp": b} for a, b in group] + hidden_peers(hidden))
    copies = []
    own = dp * n_role + role
    for slot, (a, b) in enumerate(group):
        copies.append(
            remote(tok.at[a * n_dp + b], tok_all.at[own], (s0, r0), slot, {"role": a, "dp": b})
        )
    for slot, peer in enumerate(dp_peers(n_dp)):
        copies.append(remote(up.at[role * n_dp + peer["dp"]], up_all.at[dp], (s1, r1), slot, peer))
    for slot, peer in enumerate(hidden_peers(hidden)):
        copies.append(remote(red, red_all.at[me], (s2, r2), slot, peer))
    for copy in copies:
        copy.start()
    tok_all[own] = tok[role * n_dp + dp]
    up_all[dp] = up[role * n_dp + dp]
    red_all[me] = red[...]
    for copy in copies:
        copy.wait()


def reduce_kernel(sizes, part, grad, base, grad_sum, got, got_grad, out_part, out_grad, far, far_grad,
                  s0, r0, s1, r1, s2, r2, s3, r3):
    n_role, n_dp, _ = sizes
    role, dp = lax.axis_index("role"), lax.axis_index("dp")
    greet(dp_peers(n_dp) + [other_role()])
    copies = []
    for slot, peer in enumerate(dp_peers(n_dp)):
        copies.append(remote(part.at[:, peer["dp"]], got.at[slot], (s0, r0), slot, peer))
        copies.append(remote(grad.at[peer["dp"]], got_grad.at[slot], (s1, r1), slot, peer))
    for copy in copies:
        copy.start()
    for copy in copies:
        copy.wait()
    rows = base.shape[1]
    step = 16

    @pl.loop(0, rows // step)
    def _(i):
        at = pl.ds(pl.multiple_of(i * step, step), step)
        for k in range(2):
            total = part[k, dp, 1 - role, at].astype(F32)
            for slot in range(n_dp - 1):
                total = total + got[slot, k, 1 - role, at].astype(F32)
            out_part[k, at] = total.astype(BF16)
        total = grad[dp, at].astype(F32)
        for slot in range(n_dp - 1):
            total = total + got_grad[slot, at].astype(F32)
        out_grad[at] = total.astype(BF16)

    across = remote(out_part, far, (s2, r2), 0, other_role())
    across_grad = remote(out_grad, far_grad, (s3, r3), 0, other_role())
    across.start()

    @pl.when(role == 1)
    def _():
        across_grad.start()
        across_grad.wait_send()

    @pl.when(role == 0)
    def _():
        across_grad.wait_recv()

    across.wait()
    keep = jnp.where(role == 0, 1.0, 0.0).astype(F32)

    @pl.loop(0, rows // step)
    def _(i):
        at = pl.ds(pl.multiple_of(i * step, step), step)
        for k in range(2):
            total = part[k, dp, role, at].astype(F32)
            for slot in range(n_dp - 1):
                total = total + got[slot, k, role, at].astype(F32)
            base[k, at] = total + far[k, at].astype(F32)

        @pl.when(role == 0)
        def _():
            grad_sum[at] = out_grad[at].astype(F32) + far_grad[at].astype(F32)

        @pl.when(role == 1)
        def _():
            grad_sum[at] = jnp.zeros_like(grad_sum[at])


def share_kernel(sizes, with_hidden, with_gather, with_grad, *refs):
    n_role, n_dp, hidden = sizes
    role, dp, me = (lax.axis_index(a) for a in ("role", "dp", "hidden"))
    refs = list(refs)
    n_jobs = with_hidden + with_gather + with_grad
    ins, outs, sems = refs[:n_jobs], refs[n_jobs : 2 * n_jobs], refs[2 * n_jobs :]
    peers = []
    if with_hidden:
        peers += hidden_peers(hidden)
    if with_gather or with_grad:
        peers += dp_peers(n_dp) + [other_role()]
    greet(peers)
    waits = []
    if with_hidden:
        src, dst, pair = ins.pop(0), outs.pop(0), (sems.pop(0), sems.pop(0))
        for slot, peer in enumerate(hidden_peers(hidden)):
            copy = remote(src, dst.at[me], pair, slot, peer)
            copy.start()
            waits.append(copy)
        dst[me] = src[...]
    if with_grad:
        grad_src, grad_dst = ins.pop(), outs.pop()
        g_near, g_far = (sems.pop(-2), sems.pop()), (sems.pop(-2), sems.pop())
        grad_over = remote(grad_src, grad_dst.at[dp], g_far, 0, other_role())

        @pl.when(role == 0)
        def _():
            grad_over.start()
            grad_dst[dp] = grad_src[...]

    if with_gather:
        src, dst = ins.pop(0), outs.pop(0)
        near, far = (sems.pop(0), sems.pop(0)), (sems.pop(0), sems.pop(0))
        over = remote(src, dst.at[dp, role], far, 0, other_role())
        over.start()
        dst[dp, role] = src[...]
    if with_grad:

        @pl.when(role == 0)
        def _():
            grad_over.wait_send()

        @pl.when(role == 1)
        def _():
            grad_over.wait_recv()

        for slot, peer in enumerate(dp_peers(n_dp)):
            copy = remote(grad_dst.at[dp], grad_dst.at[dp], g_near, slot, peer)
            copy.start()
            waits.append(copy)
    if with_gather:
        over.wait()
        for slot, peer in enumerate(dp_peers(n_dp)):
            copy = remote(dst.at[dp], dst.at[dp], near, slot, peer)
            copy.start()
            waits.append(copy)
    for copy in waits:
        copy.wait()


def share(sizes, cid, hidden_in=None, gather_in=None, grad_in=None):
    n_role, n_dp, hidden = sizes
    operands, outs, scratch = [], [], []
    if hidden_in is not None:
        operands.append(hidden_in)
        outs.append(shape_of((hidden,) + hidden_in.shape, hidden_in.dtype))
        scratch += dma_pair(hidden - 1)
    if gather_in is not None:
        operands.append(gather_in)
        outs.append(shape_of((n_dp, n_role) + gather_in.shape, gather_in.dtype))
        scratch += dma_pair(n_dp - 1) + dma_pair(1)
    if grad_in is not None:
        operands.append(grad_in)
        outs.append(shape_of((n_dp,) + grad_in.shape, grad_in.dtype))
        scratch += dma_pair(1) + dma_pair(n_dp - 1)
    body = functools.partial(
        share_kernel, sizes, hidden_in is not None, gather_in is not None, grad_in is not None
    )
    return call(body, outs, scratch, cid, *operands)


def finish_kernel(sizes, with_gather, *refs):
    n_role, n_dp, hidden = sizes
    if with_gather:
        part, src, out, dst, got, summed, far, result, s0, r0, s1, r1, s2, r2, s3, r3, s4, r4 = refs
    else:
        part, out, got, summed, far, result, s0, r0, s1, r1, s2, r2 = refs
    role, dp, me = (lax.axis_index(a) for a in ("role", "dp", "hidden"))
    pairs = hidden // 2
    pair, odd = me // 2, lax.rem(me, 2)
    mine = role * n_dp + dp
    t_role, t_dp = pair // n_dp, lax.rem(pair, n_dp)
    owner = {"role": t_role, "dp": t_dp, "hidden": mine * 2 + odd}
    others = [{"hidden": ring(pair, step, pairs) * 2 + odd} for step in range(1, pairs)]
    mate = {"hidden": pair * 2 + 1 - odd}
    barrier = pltpu.get_barrier_semaphore()
    peers = others + [mate]
    if with_gather:
        peers = peers + dp_peers(n_dp) + [other_role()]
    for peer in peers:
        pl.semaphore_signal(barrier, inc=1, device_id=peer, device_id_type=MESH)

    @pl.when(mine != pair)
    def _():
        pl.semaphore_signal(barrier, inc=1, device_id=owner, device_id_type=MESH)

    pl.semaphore_wait(barrier, jnp.where(mine != pair, len(peers) + 1, len(peers)))

    if with_gather:
        over = remote(src, dst.at[dp, role], (s3, r3), 0, other_role())
        over.start()
    firsts = []
    for step in list(range(1, pairs)) + [0]:
        block = ring(pair, step, pairs)
        copy = remote(part.at[block, 1 - odd], got.at[block], (s0, r0), step, mate)
        copy.start()
        firsts.append((step, block, copy))
    if with_gather:
        dst[dp, role] = src[...]
    seconds = []
    for step, block, copy in firsts:
        copy.wait()
        total = part[block, odd].astype(F32) + got[block].astype(F32)
        summed[block] = total.astype(BF16)
        if step:
            copy = remote(summed.at[block], far.at[step - 1], (s1, r1), step - 1, others[step - 1])
            copy.start()
            seconds.append(copy)
    nears = []
    if with_gather:
        over.wait()
        for slot, peer in enumerate(dp_peers(n_dp)):
            copy = remote(dst.at[dp], dst.at[dp], (s4, r4), slot, peer)
            copy.start()
            nears.append(copy)
    total = summed[pair].astype(F32)
    for step, copy in enumerate(seconds):
        copy.wait()
        total = total + far[step].astype(F32)
    result[...] = total.astype(BF16)
    last = remote(result, out, (s2, r2), 0, owner)

    @pl.when(mine != pair)
    def _():
        last.start()
        last.wait()

    @pl.when(mine == pair)
    def _():
        out[...] = result[...]

    for copy in nears:
        copy.wait()


def finish(sizes, cid, hidden_all, down_weight, live, gather_in=None):
    n_role, n_dp, hidden = sizes
    rows = hidden_all.shape[2]
    width = down_weight.shape[1]
    per = hidden // (n_role * n_dp)
    part = jnp.einsum("grf,fd->grd", hidden_all.reshape((-1,) + hidden_all.shape[2:]), down_weight,
                      preferred_element_type=F32).astype(BF16)
    part = part.reshape(n_dp, n_role, rows, per, width // per)
    part = part.transpose(1, 0, 3, 2, 4).reshape(n_role * n_dp, per, rows, width // per)
    pairs = hidden // 2
    block = (rows, width // per)
    outs, operands, more = [shape_of(block, BF16)], [part], []
    if gather_in is not None:
        outs.append(shape_of((n_dp, n_role) + gather_in.shape, gather_in.dtype))
        operands.append(gather_in)
        more = dma_pair(1) + dma_pair(n_dp - 1)
    out, *gathered = call(
        functools.partial(finish_kernel, sizes, gather_in is not None),
        outs,
        [
            pltpu.VMEM((pairs,) + block, BF16),
            pltpu.VMEM((pairs,) + block, BF16),
            pltpu.VMEM((pairs - 1,) + block, BF16),
            pltpu.VMEM(block, BF16),
        ]
        + dma_pair(pairs)
        + dma_pair(pairs - 1)
        + dma_pair(1)
        + more,
        cid,
        *operands,
    )
    return [jnp.where(live[:, None], out, jnp.zeros_like(out))] + gathered


def local(
    sizes,
    token_rows,
    cotangent,
    staleness,
    prefill_rows,
    frozen_gate_up_weight,
    down_weight,
    adapter_in,
    adapter_out,
    moment_in,
    square_in,
    moment_out,
    square_out,
):
    n_role, n_dp, hidden = sizes
    groups = n_role * n_dp
    half_index = lax.axis_index("role")
    shard_index = lax.axis_index("hidden")
    token_batch = token_rows[0]
    rows, model = token_batch.shape
    part_width = adapter_in.shape[1]
    rank = adapter_in.shape[2]
    units = frozen_gate_up_weight.shape[2]
    width = frozen_gate_up_weight.shape[1]
    positions = jnp.arange(rows)
    live = jnp.logical_or(half_index == 0, positions < prefill_rows[0])

    token_part = lax.dynamic_slice_in_dim(token_batch, shard_index * part_width, part_width, 1)
    reduced_part = jnp.einsum(
        "rd,kdq->kqr", token_part, adapter_in.astype(BF16), preferred_element_type=F32
    )
    row_weight = KEEP_RATE ** staleness.astype(F32)
    upstream = (row_weight[:, None] * cotangent.astype(F32)).astype(BF16)

    def blocked(value):
        return value.reshape(rows, groups, width).transpose(1, 0, 2)

    tokens_all, upstream_all, reduced_all = call(
        functools.partial(spread_kernel, sizes),
        [
            shape_of((groups, rows, width), BF16),
            shape_of((n_dp, rows, width), BF16),
            shape_of((hidden, 2, rank, rows), F32),
        ],
        dma_pair(groups - 1) + dma_pair(n_dp - 1) + dma_pair(hidden - 1),
        1,
        blocked(token_batch),
        blocked(upstream),
        reduced_part,
    )
    products = jnp.einsum(
        "rd,kdf->krf",
        tokens_all.reshape(groups * rows, width),
        frozen_gate_up_weight,
        preferred_element_type=F32,
    ).astype(BF16).reshape(2, n_dp, n_role, rows, units)
    grad_products = lax.dot_general(
        upstream_all.reshape(n_dp * rows, width),
        down_weight,
        (((1,), (1,)), ((), ())),
        preferred_element_type=F32,
    ).astype(BF16).reshape(n_dp, rows, units)
    base, grad_hidden = call(
        functools.partial(reduce_kernel, sizes),
        [shape_of((2, rows, units), F32), shape_of((rows, units), F32)],
        [
            pltpu.VMEM((n_dp - 1, 2, n_role, rows, units), BF16),
            pltpu.VMEM((n_dp - 1, rows, units), BF16),
            pltpu.VMEM((2, rows, units), BF16),
            pltpu.VMEM((rows, units), BF16),
            pltpu.VMEM((2, rows, units), BF16),
            pltpu.VMEM((rows, units), BF16),
        ]
        + dma_pair(n_dp - 1)
        + dma_pair(n_dp - 1)
        + dma_pair(1)
        + dma_pair(1),
        2,
        products,
        grad_products,
    )
    reduced = reduced_all.sum(axis=0).astype(BF16)
    out_bf = adapter_out.astype(BF16)
    pre = base + ADAPTER_SCALE * jnp.einsum(
        "kqr,kqf->krf", reduced, out_bf, preferred_element_type=F32
    )
    sigma = jax.nn.sigmoid(pre[0])
    hidden_old = (pre[0] * sigma * pre[1]).astype(BF16)
    grad_gate = (grad_hidden * pre[1] * sigma * (1.0 + pre[0] * (1.0 - sigma))).astype(BF16)
    grad_up = (grad_hidden * pre[0] * sigma).astype(BF16)
    grads = jnp.stack([grad_gate, grad_up])
    partial_out = ADAPTER_SCALE * jnp.einsum(
        "kqr,krf->kqf", reduced, grads, preferred_element_type=F32
    )
    through_part = jnp.einsum("krf,kqf->kqr", grads, out_bf, preferred_element_type=F32)
    through_all, hidden_old_all = share(sizes, 3, through_part, hidden_old)
    through = through_all.sum(axis=0).astype(BF16)
    partial_in = ADAPTER_SCALE * jnp.einsum(
        "un,hju->hjn", token_part, through, preferred_element_type=F32
    )
    rank_rows = 2 * rank
    packed = jnp.concatenate(
        [partial_in.reshape(rank_rows, -1), partial_out.reshape(rank_rows, -1)], axis=1
    )
    (packed_all,) = share(sizes, 4, None, None, packed)
    grad_in_all = packed_all[:, :, :part_width].reshape(n_dp, 2, rank, part_width)
    grad_out_all = packed_all[:, :, part_width:].reshape(n_dp, 2, rank, units)
    grad_in = grad_in_all.sum(axis=0).transpose(0, 2, 1)
    grad_out = grad_out_all.sum(axis=0)
    new_in, new_m_in, new_s_in = adam_update(adapter_in, grad_in, moment_in, square_in, model)
    new_out, new_m_out, new_s_out = adam_update(
        adapter_out, grad_out, moment_out, square_out, model
    )
    new_part = jnp.einsum(
        "rd,kdq->kqr", token_part, new_in.astype(BF16), preferred_element_type=F32
    )
    (new_all,) = share(sizes, 5, new_part)
    new_reduced = new_all.sum(axis=0).astype(BF16)
    post = base + ADAPTER_SCALE * jnp.einsum(
        "kqr,kqf->krf", new_reduced, new_out.astype(BF16), preferred_element_type=F32
    )
    hidden_new = (jax.nn.silu(post[0]) * post[1]).astype(BF16)
    layer_old, hidden_new_all = finish(sizes, 7, hidden_old_all, down_weight, live, hidden_new)
    (layer_new,) = finish(sizes, 8, hidden_new_all, down_weight, live)
    return (
        layer_old[None],
        layer_new[None],
        new_in[None],
        new_out[None],
        new_m_in[None],
        new_s_in[None],
        new_m_out[None],
        new_s_out[None],
    )


def solution(mesh):
    in_specs = (
        P("role", "dp", None),
        P("dp", None),
        P("dp"),
        P("dp"),
        P(None, ("role", "dp"), "hidden"),
        P("hidden", ("role", "dp")),
        P(None, "hidden", None),
        P(None, None, "hidden"),
        P(None, "hidden", None),
        P(None, "hidden", None),
        P(None, None, "hidden"),
        P(None, None, "hidden"),
    )
    out_specs = (
        P("role", "dp", "hidden"),
        P("role", "dp", "hidden"),
        P("role", None, "hidden", None),
        P("role", None, None, "hidden"),
        P("role", None, "hidden", None),
        P("role", None, "hidden", None),
        P("role", None, None, "hidden"),
        P("role", None, None, "hidden"),
    )
    sizes = tuple(mesh.shape[axis] for axis in ("role", "dp", "hidden"))
    return jax.shard_map(
        functools.partial(local, sizes),
        mesh=mesh,
        in_specs=in_specs,
        out_specs=out_specs,
        check_vma=False,
    )
```

```python
import functools

import jax
import jax.numpy as jnp
from jax import lax
from jax.experimental import pallas as pl
from jax.experimental.pallas import tpu as pltpu
from jax.sharding import PartitionSpec as P

OPT_STEP = 10
ADAPTER_SCALE = 2.0
BETA_ONE = 0.9
BETA_TWO = 0.999
RATE_FACTOR = 0.34
ADAM_EPS = 1e-08
KEEP_RATE = 0.75

MESH = pl.DeviceIdType.MESH
VMEM_LIMIT = 48 * 1024 * 1024
F32 = jnp.float32
BF16 = jnp.bfloat16


def adam_update(param, grad, first, second, width):
    learn_rate = RATE_FACTOR / width**0.5
    first_new = BETA_ONE * first + (1.0 - BETA_ONE) * grad
    second_new = BETA_TWO * second + (1.0 - BETA_TWO) * grad * grad
    first_fix = first_new / (1.0 - BETA_ONE**OPT_STEP)
    second_fix = second_new / (1.0 - BETA_TWO**OPT_STEP)
    return (
        param - learn_rate * first_fix / (jnp.sqrt(second_fix) + ADAM_EPS),
        first_new,
        second_new,
    )


def shape_of(shape, dtype):
    return jax.ShapeDtypeStruct(shape, dtype)


def ring(index, step, size):
    return lax.rem(index + step, size)


def remote(src, dst, sems, slot, device):
    send, recv = sems
    return pltpu.make_async_remote_copy(
        src_ref=src,
        dst_ref=dst,
        send_sem=send.at[slot],
        recv_sem=recv.at[slot],
        device_id=device,
        device_id_type=MESH,
    )


def greet(peers):
    barrier = pltpu.get_barrier_semaphore()
    for peer in peers:
        pl.semaphore_signal(barrier, inc=1, device_id=peer, device_id_type=MESH)
    pl.semaphore_wait(barrier, len(peers))


def hidden_peers(hidden):
    me = lax.axis_index("hidden")
    return [{"hidden": ring(me, step, hidden)} for step in range(1, hidden)]


def dp_peers(n_dp):
    me = lax.axis_index("dp")
    return [{"dp": ring(me, step, n_dp)} for step in range(1, n_dp)]


def other_role():
    return {"role": 1 - lax.axis_index("role")}


def call(body, outs, scratch, cid, *operands, anywhere=0):
    spec = pl.BlockSpec(memory_space=pltpu.VMEM)
    return pl.pallas_call(
        body,
        out_shape=outs,
        in_specs=[spec] * (len(operands) - anywhere)
        + [pl.BlockSpec(memory_space=pl.ANY)] * anywhere,
        out_specs=[spec] * len(outs),
        scratch_shapes=scratch,
        compiler_params=pltpu.CompilerParams(
            collective_id=cid, has_side_effects=True, vmem_limit_bytes=VMEM_LIMIT
        ),
    )(*operands)


def dma_pair(count):
    return [pltpu.SemaphoreType.DMA((count,)), pltpu.SemaphoreType.DMA((count,))]


def spread_kernel(sizes, tok, up, red, tok_all, up_all, red_all, s0, r0, s1, r1, s2, r2):
    n_role, n_dp, hidden = sizes
    role, dp, me = (lax.axis_index(a) for a in ("role", "dp", "hidden"))
    group = [
        (ring(role, a, n_role), ring(dp, b, n_dp))
        for a in range(n_role)
        for b in range(n_dp)
        if a or b
    ]
    greet([{"role": a, "dp": b} for a, b in group] + hidden_peers(hidden))
    copies = []
    own = role * n_dp + dp
    for slot, (a, b) in enumerate(group):
        copies.append(
            remote(tok.at[a * n_dp + b], tok_all.at[own], (s0, r0), slot, {"role": a, "dp": b})
        )
    for slot, peer in enumerate(dp_peers(n_dp)):
        copies.append(remote(up.at[role * n_dp + peer["dp"]], up_all.at[dp], (s1, r1), slot, peer))
    for slot, peer in enumerate(hidden_peers(hidden)):
        copies.append(remote(red, red_all.at[me], (s2, r2), slot, peer))
    for copy in copies:
        copy.start()
    tok_all[own] = tok[role * n_dp + dp]
    up_all[dp] = up[role * n_dp + dp]
    red_all[me] = red[...]
    for copy in copies:
        copy.wait()


def product_kernel(sizes, tok, up, weight, down, base, grad_sum, held, held_down, theirs, ours, grads,
                   got_theirs, got_ours, got_grads, out_part, out_grad, far, far_grad, load,
                   s0, r0, s1, r1, s2, r2, s3, r3, s4, r4):
    n_role, n_dp, _ = sizes
    role, dp = lax.axis_index("role"), lax.axis_index("dp")
    rows, width = tok.shape[2], tok.shape[3]
    units = weight.shape[2]
    mates = dp_peers(n_dp)
    loads = [pltpu.make_async_copy(weight.at[k], held.at[k], load.at[k]) for k in range(2)]
    loads.append(pltpu.make_async_copy(down, held_down, load.at[2]))
    for copy in loads:
        copy.start()
    greet(mates + [other_role()])

    def product(which, k):
        left = tok[which].reshape(n_dp * rows, width)
        value = jnp.dot(left, held[k], preferred_element_type=F32)
        return value.astype(BF16).reshape(n_dp, rows, units)

    def send(src, dst, pair, first):
        copies = [
            remote(src.at[peer["dp"]], dst.at[slot], pair, first + slot, peer)
            for slot, peer in enumerate(mates)
        ]
        for copy in copies:
            copy.start()
        return copies

    def settle(copies, add):
        for copy in copies:
            copy.wait()
        step = 16

        @pl.loop(0, rows // step)
        def _(i):
            add(pl.ds(pl.multiple_of(i * step, step), step))

    def summed(mine, got, at):
        total = mine[dp, at].astype(F32)
        for slot in range(n_dp - 1):
            total = total + got[slot, at].astype(F32)
        return total

    sent = []
    for k in range(2):
        loads[k].wait()
        theirs[k] = product(1 - role, k)
        sent.append(send(theirs.at[k], got_theirs.at[k], (s0, r0), k * (n_dp - 1)))
    across = []
    for k in range(2):

        def add(at, k=k):
            out_part[k, at] = summed(theirs.at[k], got_theirs.at[k], at).astype(BF16)

        settle(sent[k], add)
        across.append(remote(out_part.at[k], far.at[k], (s2, r2), k, other_role()))
        across[k].start()
    loads[2].wait()
    value = lax.dot_general(
        up[...].reshape(n_dp * rows, width),
        held_down[...],
        (((1,), (1,)), ((), ())),
        preferred_element_type=F32,
    )
    grads[...] = value.astype(BF16).reshape(n_dp, rows, units)
    sent_grad = send(grads, got_grads, (s1, r1), 0)
    sent = []
    for k in range(2):
        ours[k] = product(role, k)
        sent.append(send(ours.at[k], got_ours.at[k], (s4, r4), k * (n_dp - 1)))

    def add_grad(at):
        out_grad[at] = summed(grads, got_grads, at).astype(BF16)

    settle(sent_grad, add_grad)
    across_grad = remote(out_grad, far_grad, (s3, r3), 0, other_role())

    @pl.when(role == 1)
    def _():
        across_grad.start()

    for k in range(2):

        def add_own(at, k=k):
            base[k, at] = summed(ours.at[k], got_ours.at[k], at)

        settle(sent[k], add_own)
    for k in range(2):

        def add_far(at, k=k):
            base[k, at] = base[k, at] + far[k, at].astype(F32)

        settle([across[k]], add_far)

    @pl.when(role == 1)
    def _():
        across_grad.wait_send()
        grad_sum[...] = jnp.zeros_like(grad_sum)

    @pl.when(role == 0)
    def _():
        across_grad.wait_recv()
        grad_sum[...] = out_grad[...].astype(F32) + far_grad[...].astype(F32)


def share_kernel(sizes, with_hidden, with_gather, with_grad, *refs):
    n_role, n_dp, hidden = sizes
    role, dp, me = (lax.axis_index(a) for a in ("role", "dp", "hidden"))
    refs = list(refs)
    n_jobs = with_hidden + with_gather + with_grad
    ins, outs, sems = refs[:n_jobs], refs[n_jobs : 2 * n_jobs], refs[2 * n_jobs :]
    peers = []
    if with_hidden:
        peers += hidden_peers(hidden)
    if with_gather or with_grad:
        peers += dp_peers(n_dp) + [other_role()]
    greet(peers)
    waits = []
    if with_hidden:
        src, dst, pair = ins.pop(0), outs.pop(0), (sems.pop(0), sems.pop(0))
        for slot, peer in enumerate(hidden_peers(hidden)):
            copy = remote(src, dst.at[me], pair, slot, peer)
            copy.start()
            waits.append(copy)
        dst[me] = src[...]
    if with_grad:
        grad_src, grad_dst = ins.pop(), outs.pop()
        g_near, g_far = (sems.pop(-2), sems.pop()), (sems.pop(-2), sems.pop())
        grad_over = remote(grad_src, grad_dst.at[dp], g_far, 0, other_role())

        @pl.when(role == 0)
        def _():
            grad_over.start()
            grad_dst[dp] = grad_src[...]

    if with_gather:
        src, dst = ins.pop(0), outs.pop(0)
        near, far = (sems.pop(0), sems.pop(0)), (sems.pop(0), sems.pop(0))
        over = remote(src, dst.at[dp, role], far, 0, other_role())
        over.start()
        dst[dp, role] = src[...]
    if with_grad:

        @pl.when(role == 0)
        def _():
            grad_over.wait_send()

        @pl.when(role == 1)
        def _():
            grad_over.wait_recv()

        for slot, peer in enumerate(dp_peers(n_dp)):
            copy = remote(grad_dst.at[dp], grad_dst.at[dp], g_near, slot, peer)
            copy.start()
            waits.append(copy)
    if with_gather:
        over.wait()
        for slot, peer in enumerate(dp_peers(n_dp)):
            copy = remote(dst.at[dp], dst.at[dp], near, slot, peer)
            copy.start()
            waits.append(copy)
    for copy in waits:
        copy.wait()


def share(sizes, cid, hidden_in=None, gather_in=None, grad_in=None):
    n_role, n_dp, hidden = sizes
    operands, outs, scratch = [], [], []
    if hidden_in is not None:
        operands.append(hidden_in)
        outs.append(shape_of((hidden,) + hidden_in.shape, hidden_in.dtype))
        scratch += dma_pair(hidden - 1)
    if gather_in is not None:
        operands.append(gather_in)
        outs.append(shape_of((n_dp, n_role) + gather_in.shape, gather_in.dtype))
        scratch += dma_pair(n_dp - 1) + dma_pair(1)
    if grad_in is not None:
        operands.append(grad_in)
        outs.append(shape_of((n_dp,) + grad_in.shape, grad_in.dtype))
        scratch += dma_pair(1) + dma_pair(n_dp - 1)
    body = functools.partial(
        share_kernel, sizes, hidden_in is not None, gather_in is not None, grad_in is not None
    )
    return call(body, outs, scratch, cid, *operands)


def finish_kernel(sizes, with_gather, *refs):
    n_role, n_dp, hidden = sizes
    if with_gather:
        part, src, out, dst, got, summed, far, result, s0, r0, s1, r1, s2, r2, s3, r3, s4, r4 = refs
    else:
        part, out, got, summed, far, result, s0, r0, s1, r1, s2, r2 = refs
    role, dp, me = (lax.axis_index(a) for a in ("role", "dp", "hidden"))
    pairs = hidden // 2
    pair, odd = me // 2, lax.rem(me, 2)
    mine = role * n_dp + dp
    t_role, t_dp = pair // n_dp, lax.rem(pair, n_dp)
    owner = {"role": t_role, "dp": t_dp, "hidden": mine * 2 + odd}
    others = [{"hidden": ring(pair, step, pairs) * 2 + odd} for step in range(1, pairs)]
    mate = {"hidden": pair * 2 + 1 - odd}
    barrier = pltpu.get_barrier_semaphore()
    peers = others + [mate]
    if with_gather:
        peers = peers + dp_peers(n_dp) + [other_role()]
    for peer in peers:
        pl.semaphore_signal(barrier, inc=1, device_id=peer, device_id_type=MESH)

    @pl.when(mine != pair)
    def _():
        pl.semaphore_signal(barrier, inc=1, device_id=owner, device_id_type=MESH)

    pl.semaphore_wait(barrier, jnp.where(mine != pair, len(peers) + 1, len(peers)))

    if with_gather:
        over = remote(src, dst.at[dp, role], (s3, r3), 0, other_role())
        over.start()
    firsts = []
    for step in list(range(1, pairs)) + [0]:
        block = ring(pair, step, pairs)
        copy = remote(part.at[block, 1 - odd], got.at[block], (s0, r0), step, mate)
        copy.start()
        firsts.append((step, block, copy))
    if with_gather:
        dst[dp, role] = src[...]
    seconds = []
    for step, block, copy in firsts:
        copy.wait()
        total = part[block, odd].astype(F32) + got[block].astype(F32)
        summed[block] = total.astype(BF16)
        if step:
            copy = remote(summed.at[block], far.at[step - 1], (s1, r1), step - 1, others[step - 1])
            copy.start()
            seconds.append(copy)
    nears = []
    if with_gather:
        over.wait()
        for slot, peer in enumerate(dp_peers(n_dp)):
            copy = remote(dst.at[dp], dst.at[dp], (s4, r4), slot, peer)
            copy.start()
            nears.append(copy)
    total = summed[pair].astype(F32)
    for step, copy in enumerate(seconds):
        copy.wait()
        total = total + far[step].astype(F32)
    result[...] = total.astype(BF16)
    last = remote(result, out, (s2, r2), 0, owner)

    @pl.when(mine != pair)
    def _():
        last.start()
        last.wait()

    @pl.when(mine == pair)
    def _():
        out[...] = result[...]

    for copy in nears:
        copy.wait()


def finish(sizes, cid, hidden_all, down_weight, live, gather_in=None):
    n_role, n_dp, hidden = sizes
    rows = hidden_all.shape[2]
    width = down_weight.shape[1]
    per = hidden // (n_role * n_dp)
    part = jnp.einsum("grf,fd->grd", hidden_all.reshape((-1,) + hidden_all.shape[2:]), down_weight,
                      preferred_element_type=F32).astype(BF16)
    part = part.reshape(n_dp, n_role, rows, per, width // per)
    part = part.transpose(1, 0, 3, 2, 4).reshape(n_role * n_dp, per, rows, width // per)
    pairs = hidden // 2
    block = (rows, width // per)
    outs, operands, more = [shape_of(block, BF16)], [part], []
    if gather_in is not None:
        outs.append(shape_of((n_dp, n_role) + gather_in.shape, gather_in.dtype))
        operands.append(gather_in)
        more = dma_pair(1) + dma_pair(n_dp - 1)
    out, *gathered = call(
        functools.partial(finish_kernel, sizes, gather_in is not None),
        outs,
        [
            pltpu.VMEM((pairs,) + block, BF16),
            pltpu.VMEM((pairs,) + block, BF16),
            pltpu.VMEM((pairs - 1,) + block, BF16),
            pltpu.VMEM(block, BF16),
        ]
        + dma_pair(pairs)
        + dma_pair(pairs - 1)
        + dma_pair(1)
        + more,
        cid,
        *operands,
    )
    return [jnp.where(live[:, None], out, jnp.zeros_like(out))] + gathered


def local(
    sizes,
    token_rows,
    cotangent,
    staleness,
    prefill_rows,
    frozen_gate_up_weight,
    down_weight,
    adapter_in,
    adapter_out,
    moment_in,
    square_in,
    moment_out,
    square_out,
):
    n_role, n_dp, hidden = sizes
    groups = n_role * n_dp
    half_index = lax.axis_index("role")
    shard_index = lax.axis_index("hidden")
    token_batch = token_rows[0]
    rows, model = token_batch.shape
    part_width = adapter_in.shape[1]
    rank = adapter_in.shape[2]
    units = frozen_gate_up_weight.shape[2]
    width = frozen_gate_up_weight.shape[1]
    positions = jnp.arange(rows)
    live = jnp.logical_or(half_index == 0, positions < prefill_rows[0])

    token_part = lax.dynamic_slice_in_dim(token_batch, shard_index * part_width, part_width, 1)
    reduced_part = jnp.einsum(
        "rd,kdq->kqr", token_part, adapter_in.astype(BF16), preferred_element_type=F32
    )
    row_weight = KEEP_RATE ** staleness.astype(F32)
    upstream = (row_weight[:, None] * cotangent.astype(F32)).astype(BF16)

    def blocked(value):
        return value.reshape(rows, groups, width).transpose(1, 0, 2)

    tokens_all, upstream_all, reduced_all = call(
        functools.partial(spread_kernel, sizes),
        [
            shape_of((groups, rows, width), BF16),
            shape_of((n_dp, rows, width), BF16),
            shape_of((hidden, 2, rank, rows), F32),
        ],
        dma_pair(groups - 1) + dma_pair(n_dp - 1) + dma_pair(hidden - 1),
        1,
        blocked(token_batch),
        blocked(upstream),
        reduced_part,
    )
    sum_shape = (rows, units)
    mates = n_dp - 1
    base, grad_hidden = call(
        functools.partial(product_kernel, sizes),
        [shape_of((2,) + sum_shape, F32), shape_of(sum_shape, F32)],
        [
            pltpu.VMEM((2, width, units), BF16),
            pltpu.VMEM((units, width), BF16),
            pltpu.VMEM((2, n_dp) + sum_shape, BF16),
            pltpu.VMEM((2, n_dp) + sum_shape, BF16),
            pltpu.VMEM((n_dp,) + sum_shape, BF16),
            pltpu.VMEM((2, mates) + sum_shape, BF16),
            pltpu.VMEM((2, mates) + sum_shape, BF16),
            pltpu.VMEM((mates,) + sum_shape, BF16),
            pltpu.VMEM((2,) + sum_shape, BF16),
            pltpu.VMEM(sum_shape, BF16),
            pltpu.VMEM((2,) + sum_shape, BF16),
            pltpu.VMEM(sum_shape, BF16),
            pltpu.SemaphoreType.DMA((3,)),
        ]
        + dma_pair(2 * mates)
        + dma_pair(mates)
        + dma_pair(2)
        + dma_pair(1)
        + dma_pair(2 * mates),
        2,
        tokens_all.reshape(n_role, n_dp, rows, width),
        upstream_all,
        frozen_gate_up_weight,
        down_weight,
        anywhere=2,
    )
    reduced = reduced_all.sum(axis=0).astype(BF16)
    out_bf = adapter_out.astype(BF16)
    pre = base + ADAPTER_SCALE * jnp.einsum(
        "kqr,kqf->krf", reduced, out_bf, preferred_element_type=F32
    )
    sigma = jax.nn.sigmoid(pre[0])
    hidden_old = (pre[0] * sigma * pre[1]).astype(BF16)
    grad_gate = (grad_hidden * pre[1] * sigma * (1.0 + pre[0] * (1.0 - sigma))).astype(BF16)
    grad_up = (grad_hidden * pre[0] * sigma).astype(BF16)
    grads = jnp.stack([grad_gate, grad_up])
    partial_out = ADAPTER_SCALE * jnp.einsum(
        "kqr,krf->kqf", reduced, grads, preferred_element_type=F32
    )
    through_part = jnp.einsum("krf,kqf->kqr", grads, out_bf, preferred_element_type=F32)
    through_all, hidden_old_all = share(sizes, 3, through_part, hidden_old)
    through = through_all.sum(axis=0).astype(BF16)
    partial_in = ADAPTER_SCALE * jnp.einsum(
        "un,hju->hjn", token_part, through, preferred_element_type=F32
    )
    rank_rows = 2 * rank
    packed = jnp.concatenate(
        [partial_in.reshape(rank_rows, -1), partial_out.reshape(rank_rows, -1)], axis=1
    )
    (packed_all,) = share(sizes, 4, None, None, packed)
    grad_in_all = packed_all[:, :, :part_width].reshape(n_dp, 2, rank, part_width)
    grad_out_all = packed_all[:, :, part_width:].reshape(n_dp, 2, rank, units)
    grad_in = grad_in_all.sum(axis=0).transpose(0, 2, 1)
    grad_out = grad_out_all.sum(axis=0)
    new_in, new_m_in, new_s_in = adam_update(adapter_in, grad_in, moment_in, square_in, model)
    new_out, new_m_out, new_s_out = adam_update(
        adapter_out, grad_out, moment_out, square_out, model
    )
    new_part = jnp.einsum(
        "rd,kdq->kqr", token_part, new_in.astype(BF16), preferred_element_type=F32
    )
    (new_all,) = share(sizes, 5, new_part)
    new_reduced = new_all.sum(axis=0).astype(BF16)
    post = base + ADAPTER_SCALE * jnp.einsum(
        "kqr,kqf->krf", new_reduced, new_out.astype(BF16), preferred_element_type=F32
    )
    hidden_new = (jax.nn.silu(post[0]) * post[1]).astype(BF16)
    layer_old, hidden_new_all = finish(sizes, 7, hidden_old_all, down_weight, live, hidden_new)
    (layer_new,) = finish(sizes, 8, hidden_new_all, down_weight, live)
    return (
        layer_old[None],
        layer_new[None],
        new_in[None],
        new_out[None],
        new_m_in[None],
        new_s_in[None],
        new_m_out[None],
        new_s_out[None],
    )


def solution(mesh):
    in_specs = (
        P("role", "dp", None),
        P("dp", None),
        P("dp"),
        P("dp"),
        P(None, ("role", "dp"), "hidden"),
        P("hidden", ("role", "dp")),
        P(None, "hidden", None),
        P(None, None, "hidden"),
        P(None, "hidden", None),
        P(None, "hidden", None),
        P(None, None, "hidden"),
        P(None, None, "hidden"),
    )
    out_specs = (
        P("role", "dp", "hidden"),
        P("role", "dp", "hidden"),
        P("role", None, "hidden", None),
        P("role", None, None, "hidden"),
        P("role", None, "hidden", None),
        P("role", None, "hidden", None),
        P("role", None, None, "hidden"),
        P("role", None, None, "hidden"),
    )
    sizes = tuple(mesh.shape[axis] for axis in ("role", "dp", "hidden"))
    return jax.shard_map(
        functools.partial(local, sizes),
        mesh=mesh,
        in_specs=in_specs,
        out_specs=out_specs,
        check_vma=False,
    )
```

```python
import functools

import jax
import jax.numpy as jnp
from jax import lax
from jax.experimental import pallas as pl
from jax.experimental.pallas import tpu as pltpu
from jax.sharding import PartitionSpec as P

OPT_STEP = 10
ADAPTER_SCALE = 2.0
BETA_ONE = 0.9
BETA_TWO = 0.999
RATE_FACTOR = 0.34
ADAM_EPS = 1e-08
KEEP_RATE = 0.75

MESH = pl.DeviceIdType.MESH
VMEM_LIMIT = 48 * 1024 * 1024
F32 = jnp.float32
BF16 = jnp.bfloat16


def adam_update(param, grad, first, second, width):
    learn_rate = RATE_FACTOR / width**0.5
    first_new = BETA_ONE * first + (1.0 - BETA_ONE) * grad
    second_new = BETA_TWO * second + (1.0 - BETA_TWO) * grad * grad
    first_fix = first_new / (1.0 - BETA_ONE**OPT_STEP)
    second_fix = second_new / (1.0 - BETA_TWO**OPT_STEP)
    return (
        param - learn_rate * first_fix / (jnp.sqrt(second_fix) + ADAM_EPS),
        first_new,
        second_new,
    )


def shape_of(shape, dtype):
    return jax.ShapeDtypeStruct(shape, dtype)


def ring(index, step, size):
    return lax.rem(index + step, size)


def remote(src, dst, sems, slot, device):
    send, recv = sems
    return pltpu.make_async_remote_copy(
        src_ref=src,
        dst_ref=dst,
        send_sem=send.at[slot],
        recv_sem=recv.at[slot],
        device_id=device,
        device_id_type=MESH,
    )


def greet(peers):
    barrier = pltpu.get_barrier_semaphore()
    for peer in peers:
        pl.semaphore_signal(barrier, inc=1, device_id=peer, device_id_type=MESH)
    pl.semaphore_wait(barrier, len(peers))


def hidden_peers(hidden):
    me = lax.axis_index("hidden")
    return [{"hidden": ring(me, step, hidden)} for step in range(1, hidden)]


def dp_peers(n_dp):
    me = lax.axis_index("dp")
    return [{"dp": ring(me, step, n_dp)} for step in range(1, n_dp)]


def other_role():
    return {"role": 1 - lax.axis_index("role")}


def call(body, outs, scratch, cid, *operands, anywhere=0):
    spec = pl.BlockSpec(memory_space=pltpu.VMEM)
    return pl.pallas_call(
        body,
        out_shape=outs,
        in_specs=[spec] * (len(operands) - anywhere)
        + [pl.BlockSpec(memory_space=pl.ANY)] * anywhere,
        out_specs=[spec] * len(outs),
        scratch_shapes=scratch,
        compiler_params=pltpu.CompilerParams(
            collective_id=cid, has_side_effects=True, vmem_limit_bytes=VMEM_LIMIT
        ),
    )(*operands)


def dma_pair(count):
    return [pltpu.SemaphoreType.DMA((count,)), pltpu.SemaphoreType.DMA((count,))]


def spread_kernel(sizes, tok, up, red, tok_all, up_all, red_all, s0, r0, s1, r1, s2, r2):
    n_role, n_dp, hidden = sizes
    role, dp, me = (lax.axis_index(a) for a in ("role", "dp", "hidden"))
    group = [
        (ring(role, a, n_role), ring(dp, b, n_dp))
        for a in range(n_role)
        for b in range(n_dp)
        if a or b
    ]
    greet([{"role": a, "dp": b} for a, b in group] + hidden_peers(hidden))
    copies = []
    own = role * n_dp + dp
    for slot, (a, b) in enumerate(group):
        copies.append(
            remote(tok.at[a * n_dp + b], tok_all.at[own], (s0, r0), slot, {"role": a, "dp": b})
        )
    for slot, peer in enumerate(dp_peers(n_dp)):
        copies.append(remote(up.at[role * n_dp + peer["dp"]], up_all.at[dp], (s1, r1), slot, peer))
    for slot, peer in enumerate(hidden_peers(hidden)):
        copies.append(remote(red, red_all.at[me], (s2, r2), slot, peer))
    for copy in copies:
        copy.start()
    tok_all[own] = tok[role * n_dp + dp]
    up_all[dp] = up[role * n_dp + dp]
    red_all[me] = red[...]
    for copy in copies:
        copy.wait()


def product_kernel(sizes, tok, up, weight, down, base, grad_sum, held, held_down, theirs, ours, grads,
                   got_theirs, got_ours, got_grads, out_part, out_grad, far, far_grad, load,
                   s0, r0, s1, r1, s2, r2, s3, r3, s4, r4):
    n_role, n_dp, _ = sizes
    role, dp = lax.axis_index("role"), lax.axis_index("dp")
    rows, width = tok.shape[2], tok.shape[3]
    units = weight.shape[1]
    mates = dp_peers(n_dp)
    loads = [pltpu.make_async_copy(weight.at[k], held.at[k], load.at[k]) for k in range(2)]
    loads.append(pltpu.make_async_copy(down, held_down, load.at[2]))
    for copy in loads:
        copy.start()
    greet(mates + [other_role()])

    def product(which, k):
        left = tok[which].reshape(n_dp * rows, width)
        value = lax.dot_general(
            left, held[k], (((1,), (1,)), ((), ())), preferred_element_type=F32
        )
        return value.astype(BF16).reshape(n_dp, rows, units)

    def send(src, dst, pair, first):
        copies = [
            remote(src.at[peer["dp"]], dst.at[slot], pair, first + slot, peer)
            for slot, peer in enumerate(mates)
        ]
        for copy in copies:
            copy.start()
        return copies

    def settle(copies, add):
        for copy in copies:
            copy.wait()
        step = 16

        @pl.loop(0, rows // step)
        def _(i):
            add(pl.ds(pl.multiple_of(i * step, step), step))

    def summed(mine, got, at):
        total = mine[dp, at].astype(F32)
        for slot in range(n_dp - 1):
            total = total + got[slot, at].astype(F32)
        return total

    sent = []
    for k in range(2):
        loads[k].wait()
        theirs[k] = product(1 - role, k)
        sent.append(send(theirs.at[k], got_theirs.at[k], (s0, r0), k * (n_dp - 1)))
    across = []
    for k in range(2):

        def add(at, k=k):
            out_part[k, at] = summed(theirs.at[k], got_theirs.at[k], at).astype(BF16)

        settle(sent[k], add)
        across.append(remote(out_part.at[k], far.at[k], (s2, r2), k, other_role()))
        across[k].start()
    loads[2].wait()
    value = lax.dot_general(
        up[...].reshape(n_dp * rows, width),
        held_down[...],
        (((1,), (1,)), ((), ())),
        preferred_element_type=F32,
    )
    grads[...] = value.astype(BF16).reshape(n_dp, rows, units)
    sent_grad = send(grads, got_grads, (s1, r1), 0)
    sent = []
    for k in range(2):
        ours[k] = product(role, k)
        sent.append(send(ours.at[k], got_ours.at[k], (s4, r4), k * (n_dp - 1)))

    def add_grad(at):
        out_grad[at] = summed(grads, got_grads, at).astype(BF16)

    settle(sent_grad, add_grad)
    across_grad = remote(out_grad, far_grad, (s3, r3), 0, other_role())

    @pl.when(role == 1)
    def _():
        across_grad.start()

    for k in range(2):

        def add_own(at, k=k):
            base[k, at] = summed(ours.at[k], got_ours.at[k], at)

        settle(sent[k], add_own)
    for k in range(2):

        def add_far(at, k=k):
            base[k, at] = base[k, at] + far[k, at].astype(F32)

        settle([across[k]], add_far)

    @pl.when(role == 1)
    def _():
        across_grad.wait_send()
        grad_sum[...] = jnp.zeros_like(grad_sum)

    @pl.when(role == 0)
    def _():
        across_grad.wait_recv()
        grad_sum[...] = out_grad[...].astype(F32) + far_grad[...].astype(F32)


def share_kernel(sizes, with_hidden, with_gather, with_grad, *refs):
    n_role, n_dp, hidden = sizes
    role, dp, me = (lax.axis_index(a) for a in ("role", "dp", "hidden"))
    refs = list(refs)
    n_jobs = with_hidden + with_gather + with_grad
    ins, outs, sems = refs[:n_jobs], refs[n_jobs : 2 * n_jobs], refs[2 * n_jobs :]
    peers = []
    if with_hidden:
        peers += hidden_peers(hidden)
    if with_gather or with_grad:
        peers += dp_peers(n_dp) + [other_role()]
    greet(peers)
    waits = []
    if with_hidden:
        src, dst, pair = ins.pop(0), outs.pop(0), (sems.pop(0), sems.pop(0))
        for slot, peer in enumerate(hidden_peers(hidden)):
            copy = remote(src, dst.at[me], pair, slot, peer)
            copy.start()
            waits.append(copy)
        dst[me] = src[...]
    if with_grad:
        grad_src, grad_dst = ins.pop(), outs.pop()
        g_near, g_far = (sems.pop(-2), sems.pop()), (sems.pop(-2), sems.pop())
        grad_over = remote(grad_src, grad_dst.at[dp], g_far, 0, other_role())

        @pl.when(role == 0)
        def _():
            grad_over.start()
            grad_dst[dp] = grad_src[...]

    if with_gather:
        src, dst = ins.pop(0), outs.pop(0)
        near, far = (sems.pop(0), sems.pop(0)), (sems.pop(0), sems.pop(0))
        over = remote(src, dst.at[dp, role], far, 0, other_role())
        over.start()
        dst[dp, role] = src[...]
    if with_grad:

        @pl.when(role == 0)
        def _():
            grad_over.wait_send()

        @pl.when(role == 1)
        def _():
            grad_over.wait_recv()

        for slot, peer in enumerate(dp_peers(n_dp)):
            copy = remote(grad_dst.at[dp], grad_dst.at[dp], g_near, slot, peer)
            copy.start()
            waits.append(copy)
    if with_gather:
        over.wait()
        for slot, peer in enumerate(dp_peers(n_dp)):
            copy = remote(dst.at[dp], dst.at[dp], near, slot, peer)
            copy.start()
            waits.append(copy)
    for copy in waits:
        copy.wait()


def share(sizes, cid, hidden_in=None, gather_in=None, grad_in=None):
    n_role, n_dp, hidden = sizes
    operands, outs, scratch = [], [], []
    if hidden_in is not None:
        operands.append(hidden_in)
        outs.append(shape_of((hidden,) + hidden_in.shape, hidden_in.dtype))
        scratch += dma_pair(hidden - 1)
    if gather_in is not None:
        operands.append(gather_in)
        outs.append(shape_of((n_dp, n_role) + gather_in.shape, gather_in.dtype))
        scratch += dma_pair(n_dp - 1) + dma_pair(1)
    if grad_in is not None:
        operands.append(grad_in)
        outs.append(shape_of((n_dp,) + grad_in.shape, grad_in.dtype))
        scratch += dma_pair(1) + dma_pair(n_dp - 1)
    body = functools.partial(
        share_kernel, sizes, hidden_in is not None, gather_in is not None, grad_in is not None
    )
    return call(body, outs, scratch, cid, *operands)


def finish_kernel(sizes, with_gather, *refs):
    n_role, n_dp, hidden = sizes
    if with_gather:
        part, src, out, dst, got, summed, far, result, s0, r0, s1, r1, s2, r2, s3, r3, s4, r4 = refs
    else:
        part, out, got, summed, far, result, s0, r0, s1, r1, s2, r2 = refs
    role, dp, me = (lax.axis_index(a) for a in ("role", "dp", "hidden"))
    pairs = hidden // 2
    pair, odd = me // 2, lax.rem(me, 2)
    mine = role * n_dp + dp
    t_role, t_dp = pair // n_dp, lax.rem(pair, n_dp)
    owner = {"role": t_role, "dp": t_dp, "hidden": mine * 2 + odd}
    others = [{"hidden": ring(pair, step, pairs) * 2 + odd} for step in range(1, pairs)]
    mate = {"hidden": pair * 2 + 1 - odd}
    barrier = pltpu.get_barrier_semaphore()
    peers = others + [mate]
    if with_gather:
        peers = peers + dp_peers(n_dp) + [other_role()]
    for peer in peers:
        pl.semaphore_signal(barrier, inc=1, device_id=peer, device_id_type=MESH)

    @pl.when(mine != pair)
    def _():
        pl.semaphore_signal(barrier, inc=1, device_id=owner, device_id_type=MESH)

    pl.semaphore_wait(barrier, jnp.where(mine != pair, len(peers) + 1, len(peers)))

    if with_gather:
        over = remote(src, dst.at[dp, role], (s3, r3), 0, other_role())
        over.start()
    firsts = []
    for step in list(range(1, pairs)) + [0]:
        block = ring(pair, step, pairs)
        copy = remote(part.at[block, 1 - odd], got.at[block], (s0, r0), step, mate)
        copy.start()
        firsts.append((step, block, copy))
    if with_gather:
        dst[dp, role] = src[...]
    seconds = []
    for step, block, copy in firsts:
        copy.wait()
        total = part[block, odd].astype(F32) + got[block].astype(F32)
        summed[block] = total.astype(BF16)
        if step:
            copy = remote(summed.at[block], far.at[step - 1], (s1, r1), step - 1, others[step - 1])
            copy.start()
            seconds.append(copy)
    nears = []
    if with_gather:
        over.wait()
        for slot, peer in enumerate(dp_peers(n_dp)):
            copy = remote(dst.at[dp], dst.at[dp], (s4, r4), slot, peer)
            copy.start()
            nears.append(copy)
    total = summed[pair].astype(F32)
    for step, copy in enumerate(seconds):
        copy.wait()
        total = total + far[step].astype(F32)
    result[...] = total.astype(BF16)
    last = remote(result, out, (s2, r2), 0, owner)

    @pl.when(mine != pair)
    def _():
        last.start()
        last.wait()

    @pl.when(mine == pair)
    def _():
        out[...] = result[...]

    for copy in nears:
        copy.wait()


def finish(sizes, cid, hidden_all, down_weight, live, gather_in=None):
    n_role, n_dp, hidden = sizes
    rows = hidden_all.shape[2]
    width = down_weight.shape[1]
    per = hidden // (n_role * n_dp)
    part = jnp.einsum("grf,fd->grd", hidden_all.reshape((-1,) + hidden_all.shape[2:]), down_weight,
                      preferred_element_type=F32).astype(BF16)
    part = part.reshape(n_dp, n_role, rows, per, width // per)
    part = part.transpose(1, 0, 3, 2, 4).reshape(n_role * n_dp, per, rows, width // per)
    pairs = hidden // 2
    block = (rows, width // per)
    outs, operands, more = [shape_of(block, BF16)], [part], []
    if gather_in is not None:
        outs.append(shape_of((n_dp, n_role) + gather_in.shape, gather_in.dtype))
        operands.append(gather_in)
        more = dma_pair(1) + dma_pair(n_dp - 1)
    out, *gathered = call(
        functools.partial(finish_kernel, sizes, gather_in is not None),
        outs,
        [
            pltpu.VMEM((pairs,) + block, BF16),
            pltpu.VMEM((pairs,) + block, BF16),
            pltpu.VMEM((pairs - 1,) + block, BF16),
            pltpu.VMEM(block, BF16),
        ]
        + dma_pair(pairs)
        + dma_pair(pairs - 1)
        + dma_pair(1)
        + more,
        cid,
        *operands,
    )
    return [jnp.where(live[:, None], out, jnp.zeros_like(out))] + gathered


def local(
    sizes,
    token_rows,
    cotangent,
    staleness,
    prefill_rows,
    frozen_gate_up_weight,
    down_weight,
    adapter_in,
    adapter_out,
    moment_in,
    square_in,
    moment_out,
    square_out,
):
    n_role, n_dp, hidden = sizes
    groups = n_role * n_dp
    half_index = lax.axis_index("role")
    shard_index = lax.axis_index("hidden")
    token_batch = token_rows[0]
    rows, model = token_batch.shape
    part_width = adapter_in.shape[1]
    rank = adapter_in.shape[2]
    units = frozen_gate_up_weight.shape[2]
    width = frozen_gate_up_weight.shape[1]
    positions = jnp.arange(rows)
    live = jnp.logical_or(half_index == 0, positions < prefill_rows[0])

    token_part = lax.dynamic_slice_in_dim(token_batch, shard_index * part_width, part_width, 1)
    reduced_part = jnp.einsum(
        "rd,kdq->kqr", token_part, adapter_in.astype(BF16), preferred_element_type=F32
    )
    row_weight = KEEP_RATE ** staleness.astype(F32)
    upstream = (row_weight[:, None] * cotangent.astype(F32)).astype(BF16)

    def blocked(value):
        return value.reshape(rows, groups, width).transpose(1, 0, 2)

    tokens_all, upstream_all, reduced_all = call(
        functools.partial(spread_kernel, sizes),
        [
            shape_of((groups, rows, width), BF16),
            shape_of((n_dp, rows, width), BF16),
            shape_of((hidden, 2, rank, rows), F32),
        ],
        dma_pair(groups - 1) + dma_pair(n_dp - 1) + dma_pair(hidden - 1),
        1,
        blocked(token_batch),
        blocked(upstream),
        reduced_part,
    )
    sum_shape = (rows, units)
    mates = n_dp - 1
    base, grad_hidden = call(
        functools.partial(product_kernel, sizes),
        [shape_of((2,) + sum_shape, F32), shape_of(sum_shape, F32)],
        [
            pltpu.VMEM((2, units, width), BF16),
            pltpu.VMEM((units, width), BF16),
            pltpu.VMEM((2, n_dp) + sum_shape, BF16),
            pltpu.VMEM((2, n_dp) + sum_shape, BF16),
            pltpu.VMEM((n_dp,) + sum_shape, BF16),
            pltpu.VMEM((2, mates) + sum_shape, BF16),
            pltpu.VMEM((2, mates) + sum_shape, BF16),
            pltpu.VMEM((mates,) + sum_shape, BF16),
            pltpu.VMEM((2,) + sum_shape, BF16),
            pltpu.VMEM(sum_shape, BF16),
            pltpu.VMEM((2,) + sum_shape, BF16),
            pltpu.VMEM(sum_shape, BF16),
            pltpu.SemaphoreType.DMA((3,)),
        ]
        + dma_pair(2 * mates)
        + dma_pair(mates)
        + dma_pair(2)
        + dma_pair(1)
        + dma_pair(2 * mates),
        2,
        tokens_all.reshape(n_role, n_dp, rows, width),
        upstream_all,
        frozen_gate_up_weight.transpose(0, 2, 1),
        down_weight,
        anywhere=2,
    )
    reduced = reduced_all.sum(axis=0).astype(BF16)
    out_bf = adapter_out.astype(BF16)
    pre = base + ADAPTER_SCALE * jnp.einsum(
        "kqr,kqf->krf", reduced, out_bf, preferred_element_type=F32
    )
    sigma = jax.nn.sigmoid(pre[0])
    hidden_old = (pre[0] * sigma * pre[1]).astype(BF16)
    grad_gate = (grad_hidden * pre[1] * sigma * (1.0 + pre[0] * (1.0 - sigma))).astype(BF16)
    grad_up = (grad_hidden * pre[0] * sigma).astype(BF16)
    grads = jnp.stack([grad_gate, grad_up])
    partial_out = ADAPTER_SCALE * jnp.einsum(
        "kqr,krf->kqf", reduced, grads, preferred_element_type=F32
    )
    through_part = jnp.einsum("krf,kqf->kqr", grads, out_bf, preferred_element_type=F32)
    through_all, hidden_old_all = share(sizes, 3, through_part, hidden_old)
    through = through_all.sum(axis=0).astype(BF16)
    partial_in = ADAPTER_SCALE * jnp.einsum(
        "un,hju->hjn", token_part, through, preferred_element_type=F32
    )
    rank_rows = 2 * rank
    packed = jnp.concatenate(
        [partial_in.reshape(rank_rows, -1), partial_out.reshape(rank_rows, -1)], axis=1
    )
    (packed_all,) = share(sizes, 4, None, None, packed)
    grad_in_all = packed_all[:, :, :part_width].reshape(n_dp, 2, rank, part_width)
    grad_out_all = packed_all[:, :, part_width:].reshape(n_dp, 2, rank, units)
    grad_in = grad_in_all.sum(axis=0).transpose(0, 2, 1)
    grad_out = grad_out_all.sum(axis=0)
    new_in, new_m_in, new_s_in = adam_update(adapter_in, grad_in, moment_in, square_in, model)
    new_out, new_m_out, new_s_out = adam_update(
        adapter_out, grad_out, moment_out, square_out, model
    )
    new_part = jnp.einsum(
        "rd,kdq->kqr", token_part, new_in.astype(BF16), preferred_element_type=F32
    )
    (new_all,) = share(sizes, 5, new_part)
    new_reduced = new_all.sum(axis=0).astype(BF16)
    post = base + ADAPTER_SCALE * jnp.einsum(
        "kqr,kqf->krf", new_reduced, new_out.astype(BF16), preferred_element_type=F32
    )
    hidden_new = (jax.nn.silu(post[0]) * post[1]).astype(BF16)
    layer_old, hidden_new_all = finish(sizes, 7, hidden_old_all, down_weight, live, hidden_new)
    (layer_new,) = finish(sizes, 8, hidden_new_all, down_weight, live)
    return (
        layer_old[None],
        layer_new[None],
        new_in[None],
        new_out[None],
        new_m_in[None],
        new_s_in[None],
        new_m_out[None],
        new_s_out[None],
    )


def solution(mesh):
    in_specs = (
        P("role", "dp", None),
        P("dp", None),
        P("dp"),
        P("dp"),
        P(None, ("role", "dp"), "hidden"),
        P("hidden", ("role", "dp")),
        P(None, "hidden", None),
        P(None, None, "hidden"),
        P(None, "hidden", None),
        P(None, "hidden", None),
        P(None, None, "hidden"),
        P(None, None, "hidden"),
    )
    out_specs = (
        P("role", "dp", "hidden"),
        P("role", "dp", "hidden"),
        P("role", None, "hidden", None),
        P("role", None, None, "hidden"),
        P("role", None, "hidden", None),
        P("role", None, "hidden", None),
        P("role", None, None, "hidden"),
        P("role", None, None, "hidden"),
    )
    sizes = tuple(mesh.shape[axis] for axis in ("role", "dp", "hidden"))
    return jax.shard_map(
        functools.partial(local, sizes),
        mesh=mesh,
        in_specs=in_specs,
        out_specs=out_specs,
        check_vma=False,
    )
```
